32 devices in a mesh: replica: 1, adapter: 32 (over z, y, x, core), tensor: 1.
Axes of the slice: x: 2, y: 2, z: 4, core: 2. Of those that a mesh axis runs over, the one named last changes fastest.
Arguments:
- hidden: bfloat16 [2, 8192, 8192], P(None, ('replica', 'adapter'), 'tensor'), may hold values from -6 to 6
- request_adapter_index: int32 [8192, 1], P(('replica', 'adapter')), may hold values from 0 to 127; in each aligned block of 256 rows (0 to 255, 256 to 511, ...) at most 2 rows name the same one
- key_base_weight: bfloat16 [8192, 1024], P('tensor'), may hold values from -0.0625 to 0.0625
- adapter_down_weight: bfloat16 [128, 8192, 64], P('adapter', 'tensor'), may hold values from -0.0625 to 0.0625
- adapter_up_weight: bfloat16 [128, 64, 1024], P('adapter', None, 'tensor'), may hold values from -0.75 to 0.75
Outputs:
- adapted_keys: bfloat16 [2, 8192, 1024], P(None, ('replica', 'adapter'), 'tensor')
The draws below stay inside these ranges and needn't reach their ends.
Inputs may be any that keep to these rules, and one draw needn't show every extreme that they name: `request_adapter_index`: among the requests held by one device along `adapter`, no adapter is named more than 2 times.
All inputs are finite; a program needn't handle non-finite values.
Results may differ from the reference program's by a relative error of at most 0.005.
Values may be sent and summed in bfloat16 or wider, within the bound.
No kernel may reach another device: no remote copies, remote signals or barrier semaphores. Data moves between devices by JAX's collectives and lax.ppermute only.
A program may use at most 128 MiB of HBM per device.

```python
import math
import jax
import jax.numpy as jnp
import numpy as np
from jax import lax

MODEL_WIDTH = 8192
KEY_WIDTH = 1024
ADAPTER_RANK = 64
DECODE_STEPS = 2
MOST = 2
REQ_DEV = 256
ADAPTER_COUNT = 128
GROUP_REQUESTS = 8192
N_ADAPTER = 32


def level_of(stream_key, dims, cuts, low, top_value):
    def one(axis_at, shards_of):
        draws = jax.random.uniform(jax.random.fold_in(jax.random.fold_in(stream_key, 6), axis_at), (shards_of,), jnp.float32, low / len(cuts), top_value / len(cuts))
        return jnp.repeat(jnp.exp(draws), dims[axis_at] // shards_of).reshape((-1,) + (1,) * (len(dims) - axis_at - 1))

    loudness = one(*cuts[0])
    for cut in cuts[1:]:
        loudness = loudness * one(*cut)
    return loudness


def deal_out(own_key, own, number, rows, count, top, limit, slope):
    sequence = jax.random.permutation(own_key, count)
    crowded, usual = portions_of(count, rows * top, limit, slope, True), portions_of(count, rows * top, limit, slope, False)
    places = jnp.arange(count)

    def named(tallies, turn):
        used = int((tallies > 0).sum())
        fixed = max(1, used // 4)
        shifted = fixed + (places - fixed + turn * (used - fixed)) % max(1, count - fixed)
        return jnp.zeros((count,), jnp.int32).at[sequence[jnp.where(places < fixed, places, shifted)]].set(jnp.asarray(tallies, jnp.int32))

    tallies = jnp.where(number % 4 == 0, named(crowded, number // 4), named(usual, number - number // 4 - 1))
    mixed = jax.random.permutation(jax.random.fold_in(own, 3), count)
    donor, taker = mixed[0:count // 2 * 2:2], mixed[1:count // 2 * 2:2]
    slack = jnp.minimum(tallies[donor] - 1, limit - tallies[taker]) // 2
    slack = jnp.where((donor == sequence[0]) | (taker == sequence[0]) | (tallies[taker] == 0), 0, jnp.maximum(slack, 0))
    shifted = jax.random.randint(jax.random.fold_in(own, 4), (count // 2,), 0, 1 << 20) % (slack + 1)
    tallies = tallies.at[donor].add(-shifted).at[taker].add(shifted)
    items = jnp.searchsorted(jnp.cumsum(tallies), jnp.arange(rows * top), side="right").astype(jnp.int32)
    listing = items.reshape(top, rows).T
    listing = listing[jax.random.permutation(jax.random.fold_in(own, 1), rows)]
    turn = jax.random.randint(jax.random.fold_in(own, 2), (rows, 1), 0, top)
    return jnp.take_along_axis(listing, (jnp.arange(top)[None, :] + turn) % top, axis=1)


def portions_of(number_of, total, most, lean, full):
    portions = [(1 << 20) // math.isqrt(grade ** lean) + 1 for grade in range(1, number_of + 1)]
    largest = most if full else min(most, max(-(-total // number_of), total * portions[0] // sum(portions)))
    least = 1 if total - largest >= number_of - 1 else 0
    given, surplus = [largest] + [least] * (number_of - 1), total - largest - least * (number_of - 1)
    while surplus > 0:
        movable = [i for i in range(1, number_of) if given[i] < largest] or [i for i in range(1, number_of) if given[i] < most]
        mass, left = sum([portions[i] for i in movable]), surplus
        for i in movable:
            extra = min(most - given[i], max(1, left * portions[i] // mass), surplus)
            given[i] = given[i] + extra
            surplus = surplus - extra
    return np.array(given)


def gaussian(key, shape, scale, bound, pieces=(), held_as=jnp.bfloat16):
    drawn = jax.random.normal(key, shape, jnp.float32) * scale
    if len(pieces) > 0:
        drawn = level_of(key, shape, pieces, -0.22, 0.18) * drawn
    return jnp.clip(drawn, min=-bound, max=bound).astype(held_as)


def setup_inputs(seed: int = 0, part: int = 0) -> dict:
    seeds = jax.random.split(jax.random.key(seed), 6)
    part_keys = jax.random.split(jax.random.fold_in(seeds[5], part), 6)
    hidden = gaussian(part_keys[0], (DECODE_STEPS, GROUP_REQUESTS, MODEL_WIDTH), 1.0, 6.0, ((1, 32),))
    request_adapter_index_keys = jax.random.split(jax.random.fold_in(part_keys[1], 1), GROUP_REQUESTS // REQ_DEV)
    request_adapter_index_turns = jax.random.permutation(jax.random.fold_in(part_keys[1], 3), GROUP_REQUESTS // REQ_DEV)
    request_adapter_index = jax.vmap(lambda own, number: deal_out(jax.random.fold_in(part_keys[1], 2), own, number, REQ_DEV, ADAPTER_COUNT, 1, MOST, 2))(request_adapter_index_keys, request_adapter_index_turns).reshape((GROUP_REQUESTS, 1))
    key_base_weight = gaussian(seeds[2], (MODEL_WIDTH, KEY_WIDTH), MODEL_WIDTH ** -0.5, 0.0625)
    adapter_down_weight = gaussian(seeds[3], (ADAPTER_COUNT, MODEL_WIDTH, ADAPTER_RANK), MODEL_WIDTH ** -0.5, 0.0625, ((0, 32),))
    adapter_up_weight = gaussian(seeds[4], (ADAPTER_COUNT, ADAPTER_RANK, KEY_WIDTH), ADAPTER_RANK ** -0.5, 0.75, ((0, 32),))
    return {"hidden": hidden, "request_adapter_index": request_adapter_index, "key_base_weight": key_base_weight, "adapter_down_weight": adapter_down_weight, "adapter_up_weight": adapter_up_weight}


def reference(hidden, request_adapter_index, key_base_weight, adapter_down_weight, adapter_up_weight):
    flat_rows = hidden.reshape(DECODE_STEPS * GROUP_REQUESTS, MODEL_WIDTH)
    base_output = jnp.dot(flat_rows, key_base_weight, preferred_element_type=jnp.float32).reshape(DECODE_STEPS, GROUP_REQUESTS, KEY_WIDTH)
    selected_down = request_adapter_index[:, 0].reshape(N_ADAPTER, REQ_DEV)
    request_groups = hidden.reshape(DECODE_STEPS, N_ADAPTER, REQ_DEV, MODEL_WIDTH).transpose(1, 0, 2, 3)

    def project_block(block):
        block_rows, selected_up = block
        down_weight = adapter_down_weight[selected_up].astype(jnp.float32)
        low = jnp.einsum("sid,idr->sir", block_rows.astype(jnp.float32), down_weight).astype(jnp.bfloat16)
        raised_state = adapter_up_weight[selected_up].astype(jnp.float32)
        return jnp.einsum("sir,ire->sie", low.astype(jnp.float32), raised_state).astype(jnp.bfloat16)

    adapter_output = lax.map(project_block, (request_groups, selected_down))
    adapter_output = adapter_output.transpose(1, 0, 2, 3).reshape(DECODE_STEPS, GROUP_REQUESTS, KEY_WIDTH)
    return (base_output + adapter_output.astype(jnp.float32)).astype(jnp.bfloat16)
```

```python
import functools

import jax
import jax.numpy as jnp
from jax import lax
from jax.experimental import pallas as pl
from jax.experimental.pallas import tpu as pltpu
from jax.sharding import PartitionSpec as P

MOST = 2
MIB = 1 << 20


def block_of(width, most):
    block = min(width, most)
    while width % block:
        block -= 128
    return block


def deal_kernel(steps, selected_ref, rows_ref, out_ref, deal_ref):
    requests = selected_ref.shape[1]
    slots = deal_ref.shape[0]

    @pl.when(pl.program_id(0) == 0)
    def _():
        selected = selected_ref[...]
        along = jnp.broadcast_to(selected, (requests, requests))
        first = lax.broadcasted_iota(jnp.int32, (requests, requests), 0)
        second = lax.broadcasted_iota(jnp.int32, (requests, requests), 1)
        down = jnp.sum(jnp.where(first == second, along, 0), axis=1, keepdims=True)
        before = (down == along) & (first < second)
        earlier = jnp.sum(before.astype(jnp.int32), axis=0, keepdims=True)
        start = (selected * MOST + earlier) * steps
        slot = lax.broadcasted_iota(jnp.int32, (slots, requests), 0)
        for step in range(steps):
            deal_ref[:, step * requests : (step + 1) * requests] = (
                (slot == start + step).astype(jnp.float32).astype(jnp.bfloat16)
            )

    out_ref[...] = jnp.dot(
        deal_ref[...], rows_ref[...], preferred_element_type=jnp.float32
    ).astype(jnp.bfloat16)


def deal_rows(selected, rows, steps, slots):
    count, width = rows.shape
    block = block_of(width, 1024)
    return pl.pallas_call(
        functools.partial(deal_kernel, steps),
        grid=(width // block,),
        in_specs=[
            pl.BlockSpec(selected.shape, lambda k: (0, 0)),
            pl.BlockSpec((count, block), lambda k: (0, k)),
        ],
        out_specs=pl.BlockSpec((slots, block), lambda k: (0, k)),
        out_shape=jax.ShapeDtypeStruct((slots, width), jnp.bfloat16),
        scratch_shapes=[pltpu.VMEM((slots, count), jnp.bfloat16)],
        compiler_params=pltpu.CompilerParams(vmem_limit_bytes=60 * MIB),
        cost_estimate=pl.CostEstimate(
            flops=2 * slots * count * width,
            bytes_accessed=2 * (slots + count) * width,
            transcendentals=0,
        ),
    )(selected, rows)


def own_columns(low, adapters, adapter_rows):
    rank = low.shape[1] // adapters
    row = lax.broadcasted_iota(jnp.int32, low.shape, 0)
    column = lax.broadcasted_iota(jnp.int32, low.shape, 1)
    own = (row // adapter_rows) % adapters == column // rank
    return jnp.where(own, low, 0.0).astype(jnp.bfloat16)


def term_kernel(adapters, adapter_rows, rows_ref, down_ref, up_ref, out_ref, low_ref):
    k = pl.program_id(0)

    @pl.when(k == 0)
    def _():
        low_ref[...] = jnp.zeros_like(low_ref)

    low_ref[...] += lax.dot_general(
        rows_ref[...],
        down_ref[...],
        (((1,), (0,)), ((), ())),
        preferred_element_type=jnp.float32,
    )

    @pl.when(k == pl.num_programs(0) - 1)
    def _():
        low = own_columns(low_ref[...], adapters, adapter_rows)
        out_ref[...] = jnp.dot(
            low, up_ref[...], preferred_element_type=jnp.float32
        ).astype(jnp.bfloat16)


def adapter_terms(rows, down, up, adapters, adapter_rows):
    slots, width = rows.shape
    ranks, out_width = up.shape
    block = block_of(width, 1024)
    return pl.pallas_call(
        functools.partial(term_kernel, adapters, adapter_rows),
        grid=(width // block,),
        in_specs=[
            pl.BlockSpec((slots, block), lambda k: (0, k)),
            pl.BlockSpec((block, ranks), lambda k: (k, 0)),
            pl.BlockSpec((ranks, out_width), lambda k: (0, 0)),
        ],
        out_specs=pl.BlockSpec((slots, out_width), lambda k: (0, 0)),
        out_shape=jax.ShapeDtypeStruct((slots, out_width), jnp.bfloat16),
        scratch_shapes=[pltpu.VMEM((slots, ranks), jnp.float32)],
        compiler_params=pltpu.CompilerParams(vmem_limit_bytes=60 * MIB),
        cost_estimate=pl.CostEstimate(
            flops=2 * slots * ranks * (width + out_width),
            bytes_accessed=2 * (slots + ranks) * (width + out_width),
            transcendentals=0,
        ),
    )(rows, down, up)


def finish_kernel(deal_ref, terms_ref, base_ref, out_ref):
    own = jnp.dot(deal_ref[...], terms_ref[...], preferred_element_type=jnp.float32)
    out_ref[...] = (base_ref[...] + own).astype(jnp.bfloat16)


def finish(deal_back, terms, base):
    return pl.pallas_call(
        finish_kernel,
        out_shape=jax.ShapeDtypeStruct(base.shape, jnp.bfloat16),
        compiler_params=pltpu.CompilerParams(vmem_limit_bytes=60 * MIB),
    )(deal_back, terms, base)


def per_device(
    hidden, request_adapter_index, key_base_weight, adapter_down_weight, adapter_up_weight
):
    steps, requests, width = hidden.shape
    owners = lax.axis_size("adapter")
    parts = lax.axis_size("tensor")
    adapters, _, rank = adapter_down_weight.shape
    out_width = adapter_up_weight.shape[2]
    adapter_rows = steps * MOST
    slots = owners * adapters * adapter_rows
    rows = hidden.reshape(steps * requests, width)
    selected = request_adapter_index.reshape(1, requests)

    outgoing = deal_rows(selected, rows, steps, slots)
    incoming = lax.all_to_all(outgoing, "adapter", split_axis=0, concat_axis=0, tiled=True)
    base = jnp.dot(rows, key_base_weight, preferred_element_type=jnp.float32)
    if parts > 1:
        base = lax.psum_scatter(base, "tensor", scatter_dimension=1, tiled=True)

    position = jnp.arange(requests, dtype=jnp.int32)
    before = (selected.T == selected) & (position[None, :] < position[:, None])
    earlier = jnp.sum(before.astype(jnp.int32), axis=1)
    start = (selected[0] * MOST + earlier) * steps
    slot = (start[None, :] + jnp.arange(steps, dtype=jnp.int32)[:, None]).reshape(-1)
    deal_back = (slot[:, None] == jnp.arange(slots, dtype=jnp.int32)[None, :]).astype(jnp.bfloat16)

    down = adapter_down_weight.transpose(1, 0, 2).reshape(width, adapters * rank)
    up = adapter_up_weight.reshape(adapters * rank, out_width)
    if parts > 1:
        low = jnp.dot(incoming, down, preferred_element_type=jnp.float32)
        low = own_columns(lax.psum(low, "tensor"), adapters, adapter_rows)
        terms = jnp.dot(low, up, preferred_element_type=jnp.float32).astype(jnp.bfloat16)
    else:
        terms = adapter_terms(incoming, down, up, adapters, adapter_rows)
    returned = lax.all_to_all(terms, "adapter", split_axis=0, concat_axis=0, tiled=True)
    out = finish(deal_back, returned, base)
    return out.reshape(steps, requests, out_width)


def solution(mesh):
    return jax.shard_map(
        per_device,
        mesh=mesh,
        in_specs=(
            P(None, ("replica", "adapter"), "tensor"),
            P(("replica", "adapter"), None),
            P("tensor", None),
            P("adapter", "tensor", None),
            P("adapter", None, "tensor"),
        ),
        out_specs=P(None, ("replica", "adapter"), "tensor"),
        check_vma=False,
    )
```

```python
import functools

import jax
import jax.numpy as jnp
from jax import lax
from jax.experimental import pallas as pl
from jax.experimental.pallas import tpu as pltpu
from jax.sharding import PartitionSpec as P

MOST = 2
MIB = 1 << 20


def block_of(width, most):
    block = min(width, most)
    while width % block:
        block -= 128
    return block


def deal_kernel(owners, block, selected_ref, rows_ref, out_ref, in_buf, out_buf, in_sem, out_sem):
    requests = selected_ref.shape[1]
    count, width = rows_ref.shape
    chunks = width // block
    steps = count // requests
    slots = out_ref.shape[0] // steps

    def load(k):
        part = pl.ds(k * block, block)
        return pltpu.make_async_copy(rows_ref.at[:, part], in_buf.at[:, part], in_sem.at[k])

    def store(k):
        part = pl.ds(k * block, block)
        return pltpu.make_async_copy(out_buf.at[:, part], out_ref.at[:, part], out_sem.at[k])

    for k in range(chunks):
        load(k).start()

    selected = selected_ref[...]
    along = jnp.broadcast_to(selected, (requests, requests))
    first = lax.broadcasted_iota(jnp.int32, (requests, requests), 0)
    second = lax.broadcasted_iota(jnp.int32, (requests, requests), 1)
    down = jnp.sum(jnp.where(first == second, along, 0), axis=1, keepdims=True)
    before = (down == along) & (first < second)
    earlier = jnp.sum(before.astype(jnp.int32), axis=0, keepdims=True)
    slot = lax.broadcasted_iota(jnp.int32, (slots, requests), 0)
    deal = (slot == selected * MOST + earlier).astype(jnp.float32).astype(jnp.bfloat16)

    for k in range(chunks):
        load(k).wait()
        part = slice(k * block, (k + 1) * block)
        dealt = [
            jnp.dot(
                deal,
                in_buf[step * requests : (step + 1) * requests, part],
                preferred_element_type=jnp.float32,
            ).reshape(owners, slots // owners, block)
            for step in range(steps)
        ]
        out_buf[:, part] = (
            jnp.concatenate(dealt, axis=1).reshape(slots * steps, block).astype(jnp.bfloat16)
        )
        store(k).start()
    for k in range(chunks):
        store(k).wait()


def deal_rows(selected, rows, owners, steps, slots):
    count, width = rows.shape
    block = block_of(width, 2048)
    return pl.pallas_call(
        functools.partial(deal_kernel, owners, block),
        in_specs=[
            pl.BlockSpec(memory_space=pltpu.VMEM),
            pl.BlockSpec(memory_space=pltpu.HBM),
        ],
        out_specs=pl.BlockSpec(memory_space=pltpu.HBM),
        out_shape=jax.ShapeDtypeStruct((slots, width), jnp.bfloat16),
        scratch_shapes=[
            pltpu.VMEM((count, width), jnp.bfloat16),
            pltpu.VMEM((slots, width), jnp.bfloat16),
            pltpu.SemaphoreType.DMA((width // block,)),
            pltpu.SemaphoreType.DMA((width // block,)),
        ],
        compiler_params=pltpu.CompilerParams(vmem_limit_bytes=60 * MIB),
        cost_estimate=pl.CostEstimate(
            flops=2 * slots * count * width // steps,
            bytes_accessed=2 * (slots + count) * width,
            transcendentals=0,
        ),
    )(selected, rows)


def own_columns(low, adapters):
    rank = low.shape[1] // adapters
    row = lax.broadcasted_iota(jnp.int32, low.shape, 0)
    column = lax.broadcasted_iota(jnp.int32, low.shape, 1)
    own = (row // MOST) % adapters == column // rank
    return jnp.where(own, low, 0.0).astype(jnp.bfloat16)


def term_kernel(
    adapters,
    parts,
    rows_ref,
    down_ref,
    up_ref,
    out_ref,
    rows_buf,
    down_buf,
    up_buf,
    low_ref,
    out_buf,
    rows_sem,
    down_sem,
    up_sem,
    out_sem,
):
    count = rows_ref.shape[0]
    block = count // out_sem.shape[0]
    last = len(parts) - 1

    def load(k):
        part = pl.ds(*parts[k])
        return (
            pltpu.make_async_copy(down_ref.at[part], down_buf.at[part], down_sem.at[k]),
            pltpu.make_async_copy(rows_ref.at[:, part], rows_buf.at[:, part], rows_sem.at[k]),
        )

    def store(i):
        part = pl.ds(i * block, block)
        return pltpu.make_async_copy(out_buf.at[part], out_ref.at[part], out_sem.at[i])

    load_up = pltpu.make_async_copy(up_ref, up_buf, up_sem)
    for k in range(last + 1):
        for copy in load(k):
            copy.start()
    load_up.start()
    for k, (start, size) in enumerate(parts):
        for copy in load(k):
            copy.wait()
        if k == last:
            load_up.wait()
        for i in range(count // block):
            part = slice(i * block, (i + 1) * block)
            low = jnp.dot(
                rows_buf[part, start : start + size],
                down_buf[start : start + size],
                preferred_element_type=jnp.float32,
            )
            if k > 0:
                low += low_ref[part]
            if k < last:
                low_ref[part] = low
                continue
            out_buf[part] = jnp.dot(
                own_columns(low, adapters), up_buf[...], preferred_element_type=jnp.float32
            ).astype(jnp.bfloat16)
            store(i).start()
    for i in range(count // block):
        store(i).wait()


def adapter_terms(rows, down, up, adapters):
    slots, width = rows.shape
    ranks, out_width = up.shape
    if width % 1024 == 0:
        eighths = (2, 3, 2, 1)
        ends = [sum(eighths[: k + 1]) * width // 8 for k in range(4)]
        parts = [(end - n * width // 8, n * width // 8) for end, n in zip(ends, eighths)]
    else:
        parts = [(0, width)]
    return pl.pallas_call(
        functools.partial(term_kernel, adapters, parts),
        in_specs=[pl.BlockSpec(memory_space=pltpu.HBM)] * 3,
        out_specs=pl.BlockSpec(memory_space=pltpu.HBM),
        out_shape=jax.ShapeDtypeStruct((slots, out_width), jnp.bfloat16),
        scratch_shapes=[
            pltpu.VMEM((slots, width), jnp.bfloat16),
            pltpu.VMEM((width, ranks), jnp.bfloat16),
            pltpu.VMEM((ranks, out_width), jnp.bfloat16),
            pltpu.VMEM((slots, ranks), jnp.float32),
            pltpu.VMEM((slots, out_width), jnp.bfloat16),
            pltpu.SemaphoreType.DMA((len(parts),)),
            pltpu.SemaphoreType.DMA((len(parts),)),
            pltpu.SemaphoreType.DMA,
            pltpu.SemaphoreType.DMA((2,)),
        ],
        compiler_params=pltpu.CompilerParams(vmem_limit_bytes=60 * MIB),
        cost_estimate=pl.CostEstimate(
            flops=2 * slots * ranks * (width + out_width),
            bytes_accessed=2 * (slots + ranks) * (width + out_width),
            transcendentals=0,
        ),
    )(rows, down, up)


def per_device(
    hidden, request_adapter_index, key_base_weight, adapter_down_weight, adapter_up_weight
):
    steps, requests, width = hidden.shape
    owners = lax.axis_size("adapter")
    parts = lax.axis_size("tensor")
    adapters, _, rank = adapter_down_weight.shape
    out_width = adapter_up_weight.shape[2]
    own_slots = adapters * MOST
    slots = owners * steps * own_slots
    rows = hidden.reshape(steps * requests, width)
    selected = request_adapter_index.reshape(1, requests)

    outgoing = deal_rows(selected, rows, owners, steps, slots)
    incoming = lax.all_to_all(outgoing, "adapter", split_axis=0, concat_axis=0, tiled=True)
    base = jnp.dot(rows, key_base_weight, preferred_element_type=jnp.float32)
    if parts > 1:
        base = lax.psum_scatter(base, "tensor", scatter_dimension=1, tiled=True)

    position = jnp.arange(requests, dtype=jnp.int32)
    before = (selected.T == selected) & (position[None, :] < position[:, None])
    earlier = jnp.sum(before.astype(jnp.int32), axis=1)
    place = selected[0] * MOST + earlier
    start = place // own_slots * (steps * own_slots) + place % own_slots
    slot = start[None, :] + jnp.arange(steps, dtype=jnp.int32)[:, None] * own_slots
    deal_back = slot.reshape(-1, 1) == jnp.arange(slots, dtype=jnp.int32)[None, :]
    deal_back = deal_back.astype(jnp.bfloat16)

    down = adapter_down_weight.transpose(1, 0, 2).reshape(width, adapters * rank)
    up = adapter_up_weight.reshape(adapters * rank, out_width)
    if parts > 1:
        low = jnp.dot(incoming, down, preferred_element_type=jnp.float32)
        low = own_columns(lax.psum(low, "tensor"), adapters)
        terms = jnp.dot(low, up, preferred_element_type=jnp.float32).astype(jnp.bfloat16)
    else:
        terms = adapter_terms(incoming, down, up, adapters)
    returned = lax.all_to_all(terms, "adapter", split_axis=0, concat_axis=0, tiled=True)
    base = lax.optimization_barrier(base)
    own = jnp.dot(deal_back, returned, preferred_element_type=jnp.float32)
    out = (base + own).astype(jnp.bfloat16)
    return out.reshape(steps, requests, out_width)


def solution(mesh):
    return jax.shard_map(
        per_device,
        mesh=mesh,
        in_specs=(
            P(None, ("replica", "adapter"), "tensor"),
            P(("replica", "adapter"), None),
            P("tensor", None),
            P("adapter", "tensor", None),
            P("adapter", None, "tensor"),
        ),
        out_specs=P(None, ("replica", "adapter"), "tensor"),
        check_vma=False,
    )
```

```python
import functools

import jax
import jax.numpy as jnp
from jax import lax
from jax.experimental import pallas as pl
from jax.experimental.pallas import tpu as pltpu
from jax.sharding import PartitionSpec as P

MOST = 2
MIB = 1 << 20


def block_of(width, most):
    block = min(width, most)
    while width % block:
        block -= 128
    return block


def deal_kernel(owners, block, selected_ref, rows_ref, out_ref, in_buf, out_buf, in_sem, out_sem):
    requests = selected_ref.shape[1]
    count, width = rows_ref.shape
    chunks = width // block
    steps = count // requests
    slots = out_ref.shape[0] // steps

    def load(k):
        part = pl.ds(k * block, block)
        return pltpu.make_async_copy(rows_ref.at[:, part], in_buf.at[:, part], in_sem.at[k])

    def store(k):
        part = pl.ds(k * block, block)
        return pltpu.make_async_copy(out_buf.at[:, part], out_ref.at[:, part], out_sem.at[k])

    for k in range(chunks):
        load(k).start()

    selected = selected_ref[...]
    along = jnp.broadcast_to(selected, (requests, requests))
    first = lax.broadcasted_iota(jnp.int32, (requests, requests), 0)
    second = lax.broadcasted_iota(jnp.int32, (requests, requests), 1)
    down = jnp.sum(jnp.where(first == second, along, 0), axis=1, keepdims=True)
    before = (down == along) & (first < second)
    earlier = jnp.sum(before.astype(jnp.int32), axis=0, keepdims=True)
    slot = lax.broadcasted_iota(jnp.int32, (slots, requests), 0)
    deal = (slot == selected * MOST + earlier).astype(jnp.float32).astype(jnp.bfloat16)

    for k in range(chunks):
        load(k).wait()
        part = slice(k * block, (k + 1) * block)
        dealt = [
            jnp.dot(
                deal,
                in_buf[step * requests : (step + 1) * requests, part],
                preferred_element_type=jnp.float32,
            ).reshape(owners, slots // owners, block)
            for step in range(steps)
        ]
        out_buf[:, part] = (
            jnp.concatenate(dealt, axis=1).reshape(slots * steps, block).astype(jnp.bfloat16)
        )
        store(k).start()
    for k in range(chunks):
        store(k).wait()


def deal_rows(selected, rows, owners, steps, slots):
    count, width = rows.shape
    block = block_of(width, 2048)
    return pl.pallas_call(
        functools.partial(deal_kernel, owners, block),
        in_specs=[
            pl.BlockSpec(memory_space=pltpu.VMEM),
            pl.BlockSpec(memory_space=pltpu.HBM),
        ],
        out_specs=pl.BlockSpec(memory_space=pl.ANY),
        out_shape=jax.ShapeDtypeStruct((slots, width), jnp.bfloat16),
        scratch_shapes=[
            pltpu.VMEM((count, width), jnp.bfloat16),
            pltpu.VMEM((slots, width), jnp.bfloat16),
            pltpu.SemaphoreType.DMA((width // block,)),
            pltpu.SemaphoreType.DMA((width // block,)),
        ],
        compiler_params=pltpu.CompilerParams(vmem_limit_bytes=60 * MIB),
        cost_estimate=pl.CostEstimate(
            flops=2 * slots * count * width // steps,
            bytes_accessed=2 * (slots + count) * width,
            transcendentals=0,
        ),
    )(selected, rows)


def own_columns(low, adapters):
    rank = low.shape[1] // adapters
    row = lax.broadcasted_iota(jnp.int32, low.shape, 0)
    column = lax.broadcasted_iota(jnp.int32, low.shape, 1)
    own = (row // MOST) % adapters == column // rank
    return jnp.where(own, low, 0.0).astype(jnp.bfloat16)


def term_kernel(
    adapters, selected_ref, rows_ref, down_ref, up_ref, out_ref, again_ref, out_buf, out_sem
):
    again_ref[...] = selected_ref[...]
    count = rows_ref.shape[0]
    block = count // out_sem.shape[0]

    def store(i):
        part = pl.ds(i * block, block)
        return pltpu.make_async_copy(out_buf.at[part], out_ref.at[part], out_sem.at[i])

    low = lax.dot_general(
        rows_ref[...], down_ref[...], (((1,), (1,)), ((), ())), preferred_element_type=jnp.float32
    )
    low = own_columns(low, adapters)
    for i in range(count // block):
        part = slice(i * block, (i + 1) * block)
        out_buf[part] = jnp.dot(
            low[part], up_ref[...], preferred_element_type=jnp.float32
        ).astype(jnp.bfloat16)
        store(i).start()
    for i in range(count // block):
        store(i).wait()


def adapter_terms(selected, rows, down, up, adapters):
    slots, width = rows.shape
    ranks, out_width = up.shape
    return pl.pallas_call(
        functools.partial(term_kernel, adapters),
        in_specs=[pl.BlockSpec(memory_space=pltpu.VMEM)] * 4,
        out_specs=[
            pl.BlockSpec(memory_space=pltpu.HBM),
            pl.BlockSpec(memory_space=pltpu.VMEM),
        ],
        out_shape=[
            jax.ShapeDtypeStruct((slots, out_width), jnp.bfloat16),
            jax.ShapeDtypeStruct(selected.shape, selected.dtype),
        ],
        scratch_shapes=[
            pltpu.VMEM((slots, out_width), jnp.bfloat16),
            pltpu.SemaphoreType.DMA((2,)),
        ],
        compiler_params=pltpu.CompilerParams(vmem_limit_bytes=24 * MIB),
        cost_estimate=pl.CostEstimate(
            flops=2 * slots * ranks * (width + out_width),
            bytes_accessed=2 * (slots + ranks) * (width + out_width),
            transcendentals=0,
        ),
    )(selected, rows, down, up)


def per_device(
    hidden, request_adapter_index, key_base_weight, adapter_down_weight, adapter_up_weight
):
    steps, requests, width = hidden.shape
    owners = lax.axis_size("adapter")
    parts = lax.axis_size("tensor")
    adapters, _, rank = adapter_down_weight.shape
    out_width = adapter_up_weight.shape[2]
    own_slots = adapters * MOST
    slots = owners * steps * own_slots
    rows = hidden.reshape(steps * requests, width)
    selected = request_adapter_index.reshape(1, requests)

    outgoing = deal_rows(selected, rows, owners, steps, slots)
    incoming = lax.all_to_all(outgoing, "adapter", split_axis=0, concat_axis=0, tiled=True)

    down = adapter_down_weight.transpose(0, 2, 1).reshape(adapters * rank, width)
    up = adapter_up_weight.reshape(adapters * rank, out_width)
    if parts > 1:
        low = lax.dot_general(
            incoming, down, (((1,), (1,)), ((), ())), preferred_element_type=jnp.float32
        )
        low = own_columns(lax.psum(low, "tensor"), adapters)
        terms = jnp.dot(low, up, preferred_element_type=jnp.float32).astype(jnp.bfloat16)
    else:
        terms, selected = adapter_terms(selected, incoming, down, up, adapters)

    base = jnp.dot(rows, key_base_weight, preferred_element_type=jnp.float32)
    if parts > 1:
        base = lax.psum_scatter(base, "tensor", scatter_dimension=1, tiled=True)
    position = jnp.arange(requests, dtype=jnp.int32)
    before = (selected.T == selected) & (position[None, :] < position[:, None])
    earlier = jnp.sum(before.astype(jnp.int32), axis=1)
    place = selected[0] * MOST + earlier
    start = place // own_slots * (steps * own_slots) + place % own_slots
    slot = start[None, :] + jnp.arange(steps, dtype=jnp.int32)[:, None] * own_slots
    deal_back = slot.reshape(-1, 1) == jnp.arange(slots, dtype=jnp.int32)[None, :]
    deal_back = deal_back.astype(jnp.bfloat16)

    returned = lax.all_to_all(terms, "adapter", split_axis=0, concat_axis=0, tiled=True)
    base = lax.optimization_barrier(base)
    own = jnp.dot(deal_back, returned, preferred_element_type=jnp.float32)
    out = (base + own).astype(jnp.bfloat16)
    return out.reshape(steps, requests, out_width)


def solution(mesh):
    return jax.shard_map(
        per_device,
        mesh=mesh,
        in_specs=(
            P(None, ("replica", "adapter"), "tensor"),
            P(("replica", "adapter"), None),
            P("tensor", None),
            P("adapter", "tensor", None),
            P("adapter", None, "tensor"),
        ),
        out_specs=P(None, ("replica", "adapter"), "tensor"),
        check_vma=False,
    )
```

```python
import functools

import jax
import jax.numpy as jnp
from jax import lax
from jax.experimental import pallas as pl
from jax.experimental.pallas import tpu as pltpu
from jax.sharding import PartitionSpec as P

MOST = 2
MIB = 1 << 20


def block_of(width, most):
    block = min(width, most)
    while width % block:
        block -= 128
    return block


def deal_kernel(owners, block, selected_ref, rows_ref, out_ref, in_buf, in_sem):
    requests = selected_ref.shape[1]
    count, width = rows_ref.shape
    chunks = width // block
    steps = count // requests
    slots = out_ref.shape[0] // steps

    def load(k):
        part = pl.ds(k * block, block)
        return pltpu.make_async_copy(rows_ref.at[:, part], in_buf.at[:, part], in_sem.at[k])

    for k in range(chunks):
        load(k).start()

    selected = selected_ref[...]
    along = jnp.broadcast_to(selected, (requests, requests))
    first = lax.broadcasted_iota(jnp.int32, (requests, requests), 0)
    second = lax.broadcasted_iota(jnp.int32, (requests, requests), 1)
    down = jnp.sum(jnp.where(first == second, along, 0), axis=1, keepdims=True)
    before = (down == along) & (first < second)
    earlier = jnp.sum(before.astype(jnp.int32), axis=0, keepdims=True)
    slot = lax.broadcasted_iota(jnp.int32, (slots, requests), 0)
    deal = (slot == selected * MOST + earlier).astype(jnp.float32).astype(jnp.bfloat16)

    for k in range(chunks):
        load(k).wait()
        part = slice(k * block, (k + 1) * block)
        dealt = [
            jnp.dot(
                deal,
                in_buf[step * requests : (step + 1) * requests, part],
                preferred_element_type=jnp.float32,
            ).reshape(owners, slots // owners, block)
            for step in range(steps)
        ]
        out_ref[:, part] = (
            jnp.concatenate(dealt, axis=1).reshape(slots * steps, block).astype(jnp.bfloat16)
        )


def deal_rows(selected, rows, owners, steps, slots):
    count, width = rows.shape
    block = block_of(width, 2048)
    return pl.pallas_call(
        functools.partial(deal_kernel, owners, block),
        in_specs=[
            pl.BlockSpec(memory_space=pltpu.VMEM),
            pl.BlockSpec(memory_space=pltpu.HBM),
        ],
        out_specs=pl.BlockSpec(memory_space=pltpu.VMEM),
        out_shape=jax.ShapeDtypeStruct((slots, width), jnp.bfloat16),
        scratch_shapes=[
            pltpu.VMEM((count, width), jnp.bfloat16),
            pltpu.SemaphoreType.DMA((width // block,)),
        ],
        compiler_params=pltpu.CompilerParams(vmem_limit_bytes=44 * MIB),
        cost_estimate=pl.CostEstimate(
            flops=2 * slots * count * width // steps,
            bytes_accessed=2 * (slots + count) * width,
            transcendentals=0,
        ),
    )(selected, rows)


def own_columns(low, adapters):
    rank = low.shape[1] // adapters
    row = lax.broadcasted_iota(jnp.int32, low.shape, 0)
    column = lax.broadcasted_iota(jnp.int32, low.shape, 1)
    own = (row // MOST) % adapters == column // rank
    return jnp.where(own, low, 0.0).astype(jnp.bfloat16)


def term_kernel(
    adapters, selected_ref, rows_ref, down_ref, up_ref, out_ref, again_ref, out_buf, out_sem
):
    again_ref[...] = selected_ref[...]
    count = rows_ref.shape[0]
    block = count // out_sem.shape[0]

    def store(i):
        part = pl.ds(i * block, block)
        return pltpu.make_async_copy(out_buf.at[part], out_ref.at[part], out_sem.at[i])

    low = lax.dot_general(
        rows_ref[...], down_ref[...], (((1,), (1,)), ((), ())), preferred_element_type=jnp.float32
    )
    low = own_columns(low, adapters)
    for i in range(count // block):
        part = slice(i * block, (i + 1) * block)
        out_buf[part] = jnp.dot(
            low[part], up_ref[...], preferred_element_type=jnp.float32
        ).astype(jnp.bfloat16)
        store(i).start()
    for i in range(count // block):
        store(i).wait()


def adapter_terms(selected, rows, down, up, adapters):
    slots, width = rows.shape
    ranks, out_width = up.shape
    return pl.pallas_call(
        functools.partial(term_kernel, adapters),
        in_specs=[pl.BlockSpec(memory_space=pltpu.VMEM)] * 4,
        out_specs=[
            pl.BlockSpec(memory_space=pltpu.HBM),
            pl.BlockSpec(memory_space=pltpu.VMEM),
        ],
        out_shape=[
            jax.ShapeDtypeStruct((slots, out_width), jnp.bfloat16),
            jax.ShapeDtypeStruct(selected.shape, selected.dtype),
        ],
        scratch_shapes=[
            pltpu.VMEM((slots, out_width), jnp.bfloat16),
            pltpu.SemaphoreType.DMA((2,)),
        ],
        compiler_params=pltpu.CompilerParams(vmem_limit_bytes=24 * MIB),
        cost_estimate=pl.CostEstimate(
            flops=2 * slots * ranks * (width + out_width),
            bytes_accessed=2 * (slots + ranks) * (width + out_width),
            transcendentals=0,
        ),
    )(selected, rows, down, up)


def per_device(
    hidden, request_adapter_index, key_base_weight, adapter_down_weight, adapter_up_weight
):
    steps, requests, width = hidden.shape
    owners = lax.axis_size("adapter")
    parts = lax.axis_size("tensor")
    adapters, _, rank = adapter_down_weight.shape
    out_width = adapter_up_weight.shape[2]
    own_slots = adapters * MOST
    slots = owners * steps * own_slots
    rows = hidden.reshape(steps * requests, width)
    selected = request_adapter_index.reshape(1, requests)

    outgoing = deal_rows(selected, rows, owners, steps, slots)
    incoming = lax.all_to_all(outgoing, "adapter", split_axis=0, concat_axis=0, tiled=True)

    down = adapter_down_weight.transpose(0, 2, 1).reshape(adapters * rank, width)
    up = adapter_up_weight.reshape(adapters * rank, out_width)
    if parts > 1:
        low = lax.dot_general(
            incoming, down, (((1,), (1,)), ((), ())), preferred_element_type=jnp.float32
        )
        low = own_columns(lax.psum(low, "tensor"), adapters)
        terms = jnp.dot(low, up, preferred_element_type=jnp.float32).astype(jnp.bfloat16)
    else:
        terms, selected = adapter_terms(selected, incoming, down, up, adapters)

    base = jnp.dot(rows, key_base_weight, preferred_element_type=jnp.float32)
    if parts > 1:
        base = lax.psum_scatter(base, "tensor", scatter_dimension=1, tiled=True)
    position = jnp.arange(requests, dtype=jnp.int32)
    before = (selected.T == selected) & (position[None, :] < position[:, None])
    earlier = jnp.sum(before.astype(jnp.int32), axis=1)
    place = selected[0] * MOST + earlier
    start = place // own_slots * (steps * own_slots) + place % own_slots
    slot = start[None, :] + jnp.arange(steps, dtype=jnp.int32)[:, None] * own_slots
    deal_back = slot.reshape(-1, 1) == jnp.arange(slots, dtype=jnp.int32)[None, :]
    deal_back = deal_back.astype(jnp.bfloat16)

    returned = lax.all_to_all(terms, "adapter", split_axis=0, concat_axis=0, tiled=True)
    base = lax.optimization_barrier(base)
    own = jnp.dot(deal_back, returned, preferred_element_type=jnp.float32)
    out = (base + own).astype(jnp.bfloat16)
    return out.reshape(steps, requests, out_width)


def solution(mesh):
    return jax.shard_map(
        per_device,
        mesh=mesh,
        in_specs=(
            P(None, ("replica", "adapter"), "tensor"),
            P(("replica", "adapter"), None),
            P("tensor", None),
            P("adapter", "tensor", None),
            P("adapter", None, "tensor"),
        ),
        out_specs=P(None, ("replica", "adapter"), "tensor"),
        check_vma=False,
    )
```

```python
import functools

import jax
import jax.numpy as jnp
from jax import lax
from jax.experimental import pallas as pl
from jax.experimental.pallas import tpu as pltpu
from jax.sharding import PartitionSpec as P

MOST = 2
MIB = 1 << 20
PARTS = 8


def block_of(width, most):
    block = min(width, most)
    while width % block:
        block -= 128
    return block


def deal_kernel(owners, block, selected_ref, rows_ref, after_ref, out_ref, in_buf, in_sem):
    requests = selected_ref.shape[1]
    count, width = rows_ref.shape
    chunks = width // block
    steps = count // requests
    slots = out_ref.shape[0] // steps

    def load(k):
        part = pl.ds(k * block, block)
        return pltpu.make_async_copy(rows_ref.at[:, part], in_buf.at[:, part], in_sem.at[k])

    for k in range(chunks):
        load(k).start()

    selected = selected_ref[...]
    along = jnp.broadcast_to(selected, (requests, requests))
    first = lax.broadcasted_iota(jnp.int32, (requests, requests), 0)
    second = lax.broadcasted_iota(jnp.int32, (requests, requests), 1)
    down = jnp.sum(jnp.where(first == second, along, 0), axis=1, keepdims=True)
    before = (down == along) & (first < second)
    earlier = jnp.sum(before.astype(jnp.int32), axis=0, keepdims=True)
    slot = lax.broadcasted_iota(jnp.int32, (slots, requests), 0)
    deal = (slot == selected * MOST + earlier).astype(jnp.float32).astype(jnp.bfloat16)

    for k in range(chunks):
        load(k).wait()
        part = slice(k * block, (k + 1) * block)
        dealt = [
            jnp.dot(
                deal,
                in_buf[step * requests : (step + 1) * requests, part],
                preferred_element_type=jnp.float32,
            ).reshape(owners, slots // owners, block)
            for step in range(steps)
        ]
        out_ref[:, part] = (
            jnp.concatenate(dealt, axis=1).reshape(slots * steps, block).astype(jnp.bfloat16)
        )


def deal_rows(selected, rows, after, owners, steps, slots):
    count, width = rows.shape
    block = block_of(width, 2048)
    return pl.pallas_call(
        functools.partial(deal_kernel, owners, block),
        in_specs=[
            pl.BlockSpec(memory_space=pltpu.VMEM),
            pl.BlockSpec(memory_space=pltpu.HBM),
            pl.BlockSpec(memory_space=pltpu.HBM),
        ],
        out_specs=pl.BlockSpec(memory_space=pltpu.VMEM),
        out_shape=jax.ShapeDtypeStruct((slots, width), jnp.bfloat16),
        scratch_shapes=[
            pltpu.VMEM((count, width), jnp.bfloat16),
            pltpu.SemaphoreType.DMA((width // block,)),
        ],
        compiler_params=pltpu.CompilerParams(vmem_limit_bytes=44 * MIB),
        cost_estimate=pl.CostEstimate(
            flops=2 * slots * count * width // steps,
            bytes_accessed=2 * (slots + count) * width,
            transcendentals=0,
        ),
    )(selected, rows, after)


def own_columns(low, adapters):
    rank = low.shape[1] // adapters
    row = lax.broadcasted_iota(jnp.int32, low.shape, 0)
    column = lax.broadcasted_iota(jnp.int32, low.shape, 1)
    own = (row // MOST) % adapters == column // rank
    return jnp.where(own, low, 0.0).astype(jnp.bfloat16)


def term_kernel(
    adapters,
    side_ref,
    selected_ref,
    rows_ref,
    down_ref,
    mate_down_ref,
    up_ref,
    mate_up_ref,
    out_ref,
    again_ref,
    rows_buf,
    down_buf,
    out_buf,
    rows_sem,
    down_sem,
    out_sem,
):
    again_ref[...] = selected_ref[...]
    chips, _, own_rows, width = rows_ref.shape
    mine = side_ref[0]
    sides = (mine, 1 - mine)
    downs = (down_ref, down_buf)
    ups = (up_ref, mate_up_ref)

    def pick(turn):
        return pltpu.make_async_copy(
            rows_ref.at[:, sides[turn]], rows_buf.at[turn], rows_sem.at[turn]
        )

    def store(turn):
        return pltpu.make_async_copy(
            out_buf.at[turn], out_ref.at[:, sides[turn]], out_sem.at[turn]
        )

    load = pltpu.make_async_copy(mate_down_ref, down_buf, down_sem)
    for turn in range(2):
        pick(turn).start()
    load.start()
    for turn in range(2):
        pick(turn).wait()
        if turn == 1:
            load.wait()
        low = lax.dot_general(
            rows_buf[turn].reshape(chips * own_rows, width),
            downs[turn][...],
            (((1,), (1,)), ((), ())),
            preferred_element_type=jnp.float32,
        )
        term = jnp.dot(
            own_columns(low, adapters), ups[turn][...], preferred_element_type=jnp.float32
        )
        out_buf[turn] = term.astype(jnp.bfloat16).reshape(chips, own_rows, -1)
        store(turn).start()
    for turn in range(2):
        store(turn).wait()


def adapter_terms(side, selected, rows, down, mate_down, up, mate_up, adapters):
    ranks, out_width = up.shape
    width = rows.shape[-1]
    slots = rows.size // width
    return pl.pallas_call(
        functools.partial(term_kernel, adapters),
        in_specs=[pl.BlockSpec(memory_space=pltpu.SMEM)]
        + [pl.BlockSpec(memory_space=pltpu.VMEM)] * 3
        + [pl.BlockSpec(memory_space=pltpu.HBM)]
        + [pl.BlockSpec(memory_space=pltpu.VMEM)] * 2,
        out_specs=[
            pl.BlockSpec(memory_space=pltpu.HBM),
            pl.BlockSpec(memory_space=pltpu.VMEM),
        ],
        out_shape=[
            jax.ShapeDtypeStruct(rows.shape[:-1] + (out_width,), jnp.bfloat16),
            jax.ShapeDtypeStruct(selected.shape, selected.dtype),
        ],
        scratch_shapes=[
            pltpu.VMEM((2, rows.shape[0]) + rows.shape[2:], rows.dtype),
            pltpu.VMEM(mate_down.shape, mate_down.dtype),
            pltpu.VMEM((2, rows.shape[0], rows.shape[2], out_width), rows.dtype),
            pltpu.SemaphoreType.DMA((2,)),
            pltpu.SemaphoreType.DMA,
            pltpu.SemaphoreType.DMA((2,)),
        ],
        compiler_params=pltpu.CompilerParams(vmem_limit_bytes=20 * MIB),
        cost_estimate=pl.CostEstimate(
            flops=2 * slots * ranks * (width + out_width),
            bytes_accessed=2 * (slots + 2 * ranks) * (width + out_width),
            transcendentals=0,
        ),
    )(side, selected, rows, down, mate_down, up, mate_up)


def per_device(
    hidden, request_adapter_index, key_base_weight, adapter_down_weight, adapter_up_weight
):
    steps, requests, width = hidden.shape
    owners = lax.axis_size("adapter")
    parts = lax.axis_size("tensor")
    adapters, _, rank = adapter_down_weight.shape
    out_width = adapter_up_weight.shape[2]
    own_slots = adapters * MOST
    slots = owners * steps * own_slots
    rows = hidden.reshape(steps * requests, width)
    selected = request_adapter_index.reshape(1, requests)

    side = lax.axis_index("adapter") % 2
    mates = [(i, i ^ 1) for i in range(owners)]
    teams = [list(range(0, owners, 2)), list(range(1, owners, 2))]
    down = adapter_down_weight.transpose(0, 2, 1).reshape(adapters * rank, width)
    up = adapter_up_weight.reshape(adapters * rank, out_width)
    mate_down = lax.ppermute(down, "adapter", mates)
    mate_up = lax.ppermute(up, "adapter", mates)

    def base_of_parts():
        part = width // PARTS

        def add(k, total):
            return total + jnp.dot(
                lax.dynamic_slice_in_dim(rows, k * part, part, 1),
                lax.dynamic_slice_in_dim(key_base_weight, k * part, part, 0),
                preferred_element_type=jnp.float32,
            )

        zeros = jnp.zeros((steps * requests, key_base_weight.shape[1]), jnp.float32)
        return lax.fori_loop(0, PARTS, add, zeros)

    early = lax.cond(
        side == 1,
        base_of_parts,
        lambda: jnp.zeros((steps * requests, key_base_weight.shape[1]), jnp.float32),
    )
    outgoing = deal_rows(selected, rows, early, owners, steps, slots)
    outgoing, mate_down, mate_up = lax.optimization_barrier((outgoing, mate_down, mate_up))
    incoming = lax.all_to_all(
        outgoing, "adapter", split_axis=0, concat_axis=0, tiled=True, axis_index_groups=teams
    )
    incoming = incoming.reshape(owners // 2, 2, steps * own_slots, width)
    if parts > 1:
        terms = jnp.zeros(incoming.shape[:-1] + (out_width,), jnp.bfloat16)
        for turn, (d, u) in enumerate(((down, up), (mate_down, mate_up))):
            own_side = side if turn == 0 else 1 - side
            own_in = lax.dynamic_index_in_dim(incoming, own_side, 1, keepdims=False)
            low = lax.dot_general(
                own_in.reshape(slots // 2, width),
                d,
                (((1,), (1,)), ((), ())),
                preferred_element_type=jnp.float32,
            )
            low = own_columns(lax.psum(low, "tensor"), adapters)
            term = jnp.dot(low, u, preferred_element_type=jnp.float32).astype(jnp.bfloat16)
            term = term.reshape(owners // 2, steps * own_slots, out_width)
            terms = lax.dynamic_update_index_in_dim(terms, term, own_side, 1)
    else:
        terms, selected = adapter_terms(
            side[None], selected, incoming, down, mate_down, up, mate_up, adapters
        )
    terms = terms.reshape(slots, out_width)

    position = jnp.arange(requests, dtype=jnp.int32)
    before = (selected.T == selected) & (position[None, :] < position[:, None])
    earlier = jnp.sum(before.astype(jnp.int32), axis=1)
    place = selected[0] * MOST + earlier
    start = place // own_slots * (steps * own_slots) + place % own_slots
    slot = start[None, :] + jnp.arange(steps, dtype=jnp.int32)[:, None] * own_slots
    deal_back = slot.reshape(-1, 1) == jnp.arange(slots, dtype=jnp.int32)[None, :]
    deal_back = deal_back.astype(jnp.bfloat16)

    returned = lax.all_to_all(
        terms, "adapter", split_axis=0, concat_axis=0, tiled=True, axis_index_groups=teams
    )
    own = jnp.dot(deal_back, returned, preferred_element_type=jnp.float32)
    late = lax.cond(
        side == 1,
        lambda: early,
        lambda: jnp.dot(rows, key_base_weight, preferred_element_type=jnp.float32),
    )
    base = lax.optimization_barrier(late)
    if parts > 1:
        base = lax.psum_scatter(base, "tensor", scatter_dimension=1, tiled=True)
    out = (base + own).astype(jnp.bfloat16)
    return out.reshape(steps, requests, out_width)


def solution(mesh):
    return jax.shard_map(
        per_device,
        mesh=mesh,
        in_specs=(
            P(None, ("replica", "adapter"), "tensor"),
            P(("replica", "adapter"), None),
            P("tensor", None),
            P("adapter", "tensor", None),
            P("adapter", None, "tensor"),
        ),
        out_specs=P(None, ("replica", "adapter"), "tensor"),
        check_vma=False,
    )
```

```python
import functools

import jax
import jax.numpy as jnp
from jax import lax
from jax.experimental import pallas as pl
from jax.experimental.pallas import tpu as pltpu
from jax.sharding import PartitionSpec as P

MOST = 2
MIB = 1 << 20
PARTS = 8


def block_of(width, most):
    block = min(width, most)
    while width % block:
        block -= 128
    return block


def deal_kernel(owners, block, selected_ref, rows_ref, after_ref, out_ref, in_buf, in_sem):
    requests = selected_ref.shape[1]
    count, width = rows_ref.shape
    chunks = width // block
    steps = count // requests
    slots = out_ref.shape[0] // steps

    def load(k):
        part = pl.ds(k * block, block)
        return pltpu.make_async_copy(rows_ref.at[:, part], in_buf.at[:, part], in_sem.at[k])

    for k in range(chunks):
        load(k).start()

    selected = selected_ref[...]
    along = jnp.broadcast_to(selected, (requests, requests))
    first = lax.broadcasted_iota(jnp.int32, (requests, requests), 0)
    second = lax.broadcasted_iota(jnp.int32, (requests, requests), 1)
    down = jnp.sum(jnp.where(first == second, along, 0), axis=1, keepdims=True)
    before = (down == along) & (first < second)
    earlier = jnp.sum(before.astype(jnp.int32), axis=0, keepdims=True)
    slot = lax.broadcasted_iota(jnp.int32, (slots, requests), 0)
    deal = (slot == selected * MOST + earlier).astype(jnp.float32).astype(jnp.bfloat16)

    for k in range(chunks):
        load(k).wait()
        part = slice(k * block, (k + 1) * block)
        dealt = [
            jnp.dot(
                deal,
                in_buf[step * requests : (step + 1) * requests, part],
                preferred_element_type=jnp.float32,
            ).reshape(owners, slots // owners, block)
            for step in range(steps)
        ]
        out_ref[:, part] = (
            jnp.concatenate(dealt, axis=1).reshape(slots * steps, block).astype(jnp.bfloat16)
        )


def deal_rows(selected, rows, after, owners, steps, slots):
    count, width = rows.shape
    block = block_of(width, 2048)
    return pl.pallas_call(
        functools.partial(deal_kernel, owners, block),
        in_specs=[
            pl.BlockSpec(memory_space=pltpu.VMEM),
            pl.BlockSpec(memory_space=pltpu.HBM),
            pl.BlockSpec(memory_space=pltpu.HBM),
        ],
        out_specs=pl.BlockSpec(memory_space=pltpu.VMEM),
        out_shape=jax.ShapeDtypeStruct((slots, width), jnp.bfloat16),
        scratch_shapes=[
            pltpu.VMEM((count, width), jnp.bfloat16),
            pltpu.SemaphoreType.DMA((width // block,)),
        ],
        compiler_params=pltpu.CompilerParams(vmem_limit_bytes=44 * MIB),
        cost_estimate=pl.CostEstimate(
            flops=2 * slots * count * width // steps,
            bytes_accessed=2 * (slots + count) * width,
            transcendentals=0,
        ),
    )(selected, rows, after)


def own_columns(low, adapters):
    rank = low.shape[1] // adapters
    row = lax.broadcasted_iota(jnp.int32, low.shape, 0)
    column = lax.broadcasted_iota(jnp.int32, low.shape, 1)
    own = (row // MOST) % adapters == column // rank
    return jnp.where(own, low, 0.0).astype(jnp.bfloat16)


def term_kernel(
    adapters,
    side_ref,
    selected_ref,
    rows_ref,
    down_ref,
    mate_down_ref,
    up_ref,
    mate_up_ref,
    out_ref,
    again_ref,
    down_buf,
    out_buf,
    down_sem,
    out_sem,
):
    again_ref[...] = selected_ref[...]
    chips, _, own_rows, width = rows_ref.shape
    mine = side_ref[0]
    sides = (mine, 1 - mine)
    downs = (down_ref, down_buf)
    ups = (up_ref, mate_up_ref)

    def store(turn):
        return pltpu.make_async_copy(
            out_buf.at[turn], out_ref.at[:, sides[turn]], out_sem.at[turn]
        )

    load = pltpu.make_async_copy(mate_down_ref, down_buf, down_sem)
    load.start()

    def add_terms(turn, side):
        low = lax.dot_general(
            rows_ref[:, side].reshape(chips * own_rows, width),
            downs[turn][...],
            (((1,), (1,)), ((), ())),
            preferred_element_type=jnp.float32,
        )
        term = jnp.dot(
            own_columns(low, adapters), ups[turn][...], preferred_element_type=jnp.float32
        )
        out_buf[turn] = term.astype(jnp.bfloat16).reshape(chips, own_rows, -1)
        store(turn).start()

    for turn in range(2):
        if turn == 1:
            load.wait()
        for side in range(2):
            pl.when(mine == (side + turn) % 2)(functools.partial(add_terms, turn, side))
    for turn in range(2):
        store(turn).wait()


def adapter_terms(side, selected, rows, down, mate_down, up, mate_up, adapters):
    ranks, out_width = up.shape
    width = rows.shape[-1]
    slots = rows.size // width
    return pl.pallas_call(
        functools.partial(term_kernel, adapters),
        in_specs=[pl.BlockSpec(memory_space=pltpu.SMEM)]
        + [pl.BlockSpec(memory_space=pltpu.VMEM)] * 3
        + [pl.BlockSpec(memory_space=pltpu.HBM)]
        + [pl.BlockSpec(memory_space=pltpu.VMEM)] * 2,
        out_specs=[
            pl.BlockSpec(memory_space=pltpu.HBM),
            pl.BlockSpec(memory_space=pltpu.VMEM),
        ],
        out_shape=[
            jax.ShapeDtypeStruct(rows.shape[:-1] + (out_width,), jnp.bfloat16),
            jax.ShapeDtypeStruct(selected.shape, selected.dtype),
        ],
        scratch_shapes=[
            pltpu.VMEM(mate_down.shape, mate_down.dtype),
            pltpu.VMEM((2, rows.shape[0], rows.shape[2], out_width), rows.dtype),
            pltpu.SemaphoreType.DMA,
            pltpu.SemaphoreType.DMA((2,)),
        ],
        compiler_params=pltpu.CompilerParams(vmem_limit_bytes=20 * MIB),
        cost_estimate=pl.CostEstimate(
            flops=2 * slots * ranks * (width + out_width),
            bytes_accessed=2 * (slots + 2 * ranks) * (width + out_width),
            transcendentals=0,
        ),
    )(side, selected, rows, down, mate_down, up, mate_up)


def per_device(
    hidden, request_adapter_index, key_base_weight, adapter_down_weight, adapter_up_weight
):
    steps, requests, width = hidden.shape
    owners = lax.axis_size("adapter")
    parts = lax.axis_size("tensor")
    adapters, _, rank = adapter_down_weight.shape
    out_width = adapter_up_weight.shape[2]
    own_slots = adapters * MOST
    slots = owners * steps * own_slots
    rows = hidden.reshape(steps * requests, width)
    selected = request_adapter_index.reshape(1, requests)

    side = lax.axis_index("adapter") % 2
    mates = [(i, i ^ 1) for i in range(owners)]
    teams = [list(range(0, owners, 2)), list(range(1, owners, 2))]
    down = adapter_down_weight.transpose(0, 2, 1).reshape(adapters * rank, width)
    up = adapter_up_weight.reshape(adapters * rank, out_width)
    mate_down = lax.ppermute(down, "adapter", mates)
    mate_up = lax.ppermute(up, "adapter", mates)

    def base_of_parts():
        part = width // PARTS

        def add(k, total):
            return total + jnp.dot(
                lax.dynamic_slice_in_dim(rows, k * part, part, 1),
                lax.dynamic_slice_in_dim(key_base_weight, k * part, part, 0),
                preferred_element_type=jnp.float32,
            )

        zeros = jnp.zeros((steps * requests, key_base_weight.shape[1]), jnp.float32)
        return lax.fori_loop(0, PARTS, add, zeros)

    early = lax.cond(
        side == 1,
        base_of_parts,
        lambda: jnp.zeros((steps * requests, key_base_weight.shape[1]), jnp.float32),
    )
    outgoing = deal_rows(selected, rows, early, owners, steps, slots)
    outgoing, mate_down, mate_up = lax.optimization_barrier((outgoing, mate_down, mate_up))
    incoming = lax.all_to_all(
        outgoing, "adapter", split_axis=0, concat_axis=0, tiled=True, axis_index_groups=teams
    )
    incoming = incoming.reshape(owners // 2, 2, steps * own_slots, width)
    if parts > 1:
        terms = jnp.zeros(incoming.shape[:-1] + (out_width,), jnp.bfloat16)
        for turn, (d, u) in enumerate(((down, up), (mate_down, mate_up))):
            own_side = side if turn == 0 else 1 - side
            own_in = lax.dynamic_index_in_dim(incoming, own_side, 1, keepdims=False)
            low = lax.dot_general(
                own_in.reshape(slots // 2, width),
                d,
                (((1,), (1,)), ((), ())),
                preferred_element_type=jnp.float32,
            )
            low = own_columns(lax.psum(low, "tensor"), adapters)
            term = jnp.dot(low, u, preferred_element_type=jnp.float32).astype(jnp.bfloat16)
            term = term.reshape(owners // 2, steps * own_slots, out_width)
            terms = lax.dynamic_update_index_in_dim(terms, term, own_side, 1)
    else:
        terms, selected = adapter_terms(
            side[None], selected, incoming, down, mate_down, up, mate_up, adapters
        )
    terms = terms.reshape(slots, out_width)

    position = jnp.arange(requests, dtype=jnp.int32)
    before = (selected.T == selected) & (position[None, :] < position[:, None])
    earlier = jnp.sum(before.astype(jnp.int32), axis=1)
    place = selected[0] * MOST + earlier
    start = place // own_slots * (steps * own_slots) + place % own_slots
    slot = start[None, :] + jnp.arange(steps, dtype=jnp.int32)[:, None] * own_slots
    deal_back = slot.reshape(-1, 1) == jnp.arange(slots, dtype=jnp.int32)[None, :]
    deal_back = deal_back.astype(jnp.bfloat16)

    returned = lax.all_to_all(
        terms, "adapter", split_axis=0, concat_axis=0, tiled=True, axis_index_groups=teams
    )
    own = jnp.dot(deal_back, returned, preferred_element_type=jnp.float32)
    late = lax.cond(
        side == 1,
        lambda: early,
        lambda: jnp.dot(rows, key_base_weight, preferred_element_type=jnp.float32),
    )
    base = lax.optimization_barrier(late)
    if parts > 1:
        base = lax.psum_scatter(base, "tensor", scatter_dimension=1, tiled=True)
    out = (base + own).astype(jnp.bfloat16)
    return out.reshape(steps, requests, out_width)


def solution(mesh):
    return jax.shard_map(
        per_device,
        mesh=mesh,
        in_specs=(
            P(None, ("replica", "adapter"), "tensor"),
            P(("replica", "adapter"), None),
            P("tensor", None),
            P("adapter", "tensor", None),
            P("adapter", None, "tensor"),
        ),
        out_specs=P(None, ("replica", "adapter"), "tensor"),
        check_vma=False,
    )
```
